32 devices in a mesh: grp: 2 (over y), yz: 4 (over z), gx: 4 (over x, core).
Axes of the slice: x: 2, y: 2, z: 4, core: 2. Of those that a mesh axis runs over, the one named last changes fastest.
Arguments:
- hidden: bfloat16 [32, 3, 8192], P(('grp', 'yz', 'gx')), parts along dimension 0, may hold values from -3 to 3
- cache_lengths: int32 [32], P(('grp', 'yz', 'gx')), parts along dimension 0, may hold values from 1 to 256, as said below
- image_counts: int32 [32], P(('grp', 'yz', 'gx')), parts along dimension 0, may hold values from 96 to 384, as said below
- self_keys: bfloat16 [32, 256, 1024], P(('grp', 'yz', 'gx')), parts along dimension 0, may hold values from -6 to 6
- self_values: bfloat16 [32, 256, 1024], P(('grp', 'yz', 'gx')), parts along dimension 0, may hold values from -6 to 6
- image_keys: bfloat16 [32, 384, 1024], P(('grp', 'yz', 'gx')), parts along dimension 0, may hold values from -6 to 6
- image_values: bfloat16 [32, 384, 1024], P(('grp', 'yz', 'gx')), parts along dimension 0, may hold values from -6 to 6
- norm_gain: float32 [8192], replicated, may hold values from 0.1 to 1.9
- query_weight: bfloat16 [8192, 8192], P('gx', 'yz'), may hold values from -40 to 40
- kv_weight: bfloat16 [8192, 2048], P('gx', 'yz'), may hold values from -0.0625 to 0.0625
- out_weight: bfloat16 [8192, 8192], P('gx', 'yz'), may hold values from -0.0625 to 0.0625
- cross_norm_gain: float32 [8192], replicated, may hold values from 0.1 to 1.9
- cross_query_weight: bfloat16 [8192, 8192], P('gx', 'yz'), may hold values from -0.0625 to 0.0625
- query_gain: float32 [128], replicated, may hold values from 0.1 to 160
- cross_out_weight: bfloat16 [8192, 8192], P('gx', 'yz'), may hold values from -0.0625 to 0.0625
- cross_gate: float32 [1], replicated, may hold values from 0.2 to 2
Outputs:
- layer_out: bfloat16 [32, 3, 8192], P(('grp', 'yz', 'gx')), parts along dimension 0
The draws below stay inside these ranges and needn't reach their ends.
There are 2 independent parts, one for each index of `grp`. The reference program is written for one: setup_inputs(seed, part) draws one part's arguments, and reference() takes and returns one part's arrays. A program takes and returns all parts, laid end to end along the dimension named above; an argument that names none is the same for every part. Nothing has to cross between parts.
Inputs may be any that keep to these rules, and one draw needn't show every extreme that they name: `cache_lengths`: some request has exactly 256 valid cached positions. `image_counts`: some request has exactly 384 image tokens.
All inputs are finite; a program needn't handle non-finite values.
Results may differ from the reference program's by a relative error of at most 0.0075.
The reference program's roundings to bfloat16 on the way count: a program that leaves them out, or rounds other values in their place, can miss the bound.
Values may be sent and summed in bfloat16 or wider, within the bound.
A program may use at most 128 MiB of HBM per device.

```python
import jax
import jax.numpy as jnp
from jax import lax

D = 8192
HEADS = 64
KV_HEADS = 8
HEAD_DIM = 128
DRAFT = 3
CTX = 256
IMG = 384
REQ = 16
QWIDTH = 8192
KVWIDTH = 2048


def draw_cache_lengths(key, part):
    key = jax.random.fold_in(key, 11)
    drawn = jax.random.randint(key, (REQ,), 1, CTX + 1)
    chosen = jax.random.randint(jax.random.fold_in(key, 5), (), 0, REQ)
    return jnp.where(jnp.arange(REQ) == chosen, CTX, drawn).astype(jnp.int32)


def draw_image_counts(key, part):
    key = jax.random.fold_in(key, 23)
    drawn = jax.random.randint(key, (REQ,), IMG // 4, IMG + 1)
    chosen = jax.random.randint(jax.random.fold_in(key, 7), (), 0, REQ)
    return jnp.where(jnp.arange(REQ) == chosen, IMG, drawn).astype(jnp.int32)


def draw_query_weight(key, part):
    key = jax.random.fold_in(key, 31)
    sample = jax.random.truncated_normal(key, -6.0, 6.0, (D, HEADS, HEAD_DIM), jnp.float32) * D ** (-0.5)
    return sample.reshape(D, HEADS * HEAD_DIM).astype(jnp.bfloat16)


def drawn_keys(key, slots):
    sample = jax.random.truncated_normal(key, -6.0, 6.0, (REQ, slots, KV_HEADS, HEAD_DIM), jnp.float32)
    return sample.reshape(REQ, slots, KV_HEADS * HEAD_DIM)


def draw_self_keys(key, part):
    key = jax.random.fold_in(key, 37)
    return drawn_keys(key, CTX).astype(jnp.bfloat16)


def draw_image_keys(key, part):
    key = jax.random.fold_in(key, 41)
    return drawn_keys(key, IMG).astype(jnp.bfloat16)


def draw_query_gain(key, part):
    key = jax.random.fold_in(key, 43)
    return 1.0 + 0.18 * jax.random.truncated_normal(key, -5.0, 5.0, (HEAD_DIM,), jnp.float32)


def level_of(stream_key, extent, split, low, largest):
    loudness = 1.0
    for axis_at, shards_of in split:
        steps = jax.random.uniform(jax.random.fold_in(jax.random.fold_in(stream_key, 6), axis_at), (shards_of,), jnp.float32, low / len(split), largest / len(split))
        loudness = loudness * jnp.repeat(jnp.exp(steps), extent[axis_at] // shards_of).reshape((-1,) + (1,) * (len(extent) - 1 - axis_at))
    return loudness


def noise(stream_key, extent, scale, limit, pieces=(), kind=jnp.bfloat16):
    level = level_of(stream_key, extent, pieces, -0.22, 0.18) if pieces else 1.0
    values = jax.random.normal(stream_key, extent, jnp.float32) * scale * level
    return jnp.minimum(jnp.maximum(values, -limit), limit).astype(kind)


def setup_inputs(seed: int = 0, part: int = 0) -> dict:
    arg_keys = jax.random.split(jax.random.key(seed), 17)
    part_keys = jax.random.split(jax.random.fold_in(arg_keys[16], part), 17)
    return {
        "hidden": noise(part_keys[0], (REQ, DRAFT, D), 0.5, 3.0, ((0, 16),)),
        "cache_lengths": draw_cache_lengths(jax.random.fold_in(jax.random.fold_in(arg_keys[16], part), 71), part),
        "image_counts": draw_image_counts(jax.random.fold_in(jax.random.fold_in(arg_keys[16], part), 71), part),
        "self_keys": draw_self_keys(jax.random.fold_in(jax.random.fold_in(arg_keys[16], part), 71), part),
        "self_values": noise(part_keys[4], (REQ, CTX, KVWIDTH // 2), 1.0, 6.0, ((0, 16),)),
        "image_keys": draw_image_keys(jax.random.fold_in(jax.random.fold_in(arg_keys[16], part), 71), part),
        "image_values": noise(part_keys[6], (REQ, IMG, KVWIDTH // 2), 1.0, 6.0, ((0, 16),)),
        "norm_gain": jnp.clip(1.0 + 0.18 * jax.random.normal(arg_keys[7], (D,), jnp.float32), 0.1, 1.9),
        "query_weight": draw_query_weight(jax.random.fold_in(arg_keys[16], 71), part),
        "kv_weight": noise(arg_keys[9], (D, KVWIDTH), D ** -0.5, 0.0625, ((0, 4), (1, 4))),
        "out_weight": noise(arg_keys[10], (QWIDTH, D), QWIDTH ** -0.5, 0.0625, ((0, 4), (1, 4))),
        "cross_norm_gain": jnp.clip(1.0 + 0.18 * jax.random.normal(arg_keys[11], (D,), jnp.float32), 0.1, 1.9),
        "cross_query_weight": noise(arg_keys[12], (D, QWIDTH), D ** -0.5, 0.0625, ((0, 4), (1, 4))),
        "query_gain": draw_query_gain(jax.random.fold_in(arg_keys[16], 71), part),
        "cross_out_weight": noise(arg_keys[14], (QWIDTH, D), QWIDTH ** -0.5, 0.0625, ((0, 4), (1, 4))),
        "cross_gate": jnp.clip(jax.random.uniform(arg_keys[15], (1,), jnp.float32, 0.2, 2.0), 0.2, 2.0),
    }


def rms_scale(values, gain):
    return values * lax.rsqrt(lax.optimization_barrier(jnp.mean(values * values, axis=-1, keepdims=True)) + 1e-05) * gain

def rotate(values, positions):
    half_dim = values.shape[-1] // 2
    freqs = 500000.0 ** (-2.0 * jnp.arange(half_dim, dtype=jnp.float32) / values.shape[-1])
    angles = positions.astype(jnp.float32)[:, :, None, None] * freqs
    cosine = jnp.cos(angles)
    sine = jnp.sin(angles)
    first = values[..., :half_dim]
    second = values[..., half_dim:]
    return jnp.concatenate([first * cosine - second * sine, second * cosine + first * sine], axis=-1)

def mix_heads(queries, keys, values, valid):
    requests, drafts = (queries.shape[0], queries.shape[1])
    grouped = queries.reshape(requests, drafts, KV_HEADS, HEADS // KV_HEADS, HEAD_DIM).astype(jnp.float32)
    scores = jnp.einsum('rskgd,rtkd->rkgst', grouped, keys.astype(jnp.float32)) * HEAD_DIM ** (-0.5)
    scores = jnp.where(valid[:, None, None, :, :], scores, -jnp.inf)
    highest = lax.optimization_barrier(jnp.max(scores, axis=-1, keepdims=True))
    weights = jnp.exp(scores - highest)
    probs = (weights / lax.optimization_barrier(jnp.sum(weights, axis=-1, keepdims=True))).astype(jnp.bfloat16)
    mixed = jnp.einsum('rkgst,rtkd->rskgd', probs.astype(jnp.float32), values.astype(jnp.float32))
    return mixed.astype(jnp.bfloat16).reshape(requests * drafts, HEADS * HEAD_DIM)

def reference(hidden, cache_lengths, image_counts, self_keys, self_values, image_keys, image_values, norm_gain, query_weight, kv_weight, out_weight, cross_norm_gain, cross_query_weight, query_gain, cross_out_weight, cross_gate):
    flat = hidden.reshape(REQ * DRAFT, D)
    normed = rms_scale(flat.astype(jnp.float32), norm_gain).astype(jnp.bfloat16)
    queries = jnp.dot(normed, query_weight, preferred_element_type=jnp.float32).astype(jnp.bfloat16)
    queries = queries.reshape(REQ, DRAFT, HEADS, HEAD_DIM)
    fresh = jnp.dot(normed, kv_weight, preferred_element_type=jnp.float32).astype(jnp.bfloat16)
    fresh = fresh.reshape(REQ, DRAFT, 2, KV_HEADS, HEAD_DIM)
    positions = cache_lengths[:, None] + jnp.arange(DRAFT, dtype=jnp.int32)[None, :]
    rotated = rotate(queries.astype(jnp.float32), positions).astype(jnp.bfloat16)
    new_keys = rotate(fresh[:, :, 0].astype(jnp.float32), positions).astype(jnp.bfloat16)
    all_keys = jnp.concatenate([self_keys.reshape(REQ, CTX, KV_HEADS, HEAD_DIM), new_keys], axis=1)
    all_values = jnp.concatenate([self_values.reshape(REQ, CTX, KV_HEADS, HEAD_DIM), fresh[:, :, 1]], axis=1)
    stored_valid = jnp.arange(CTX, dtype=jnp.int32)[None, None, :] < cache_lengths[:, None, None]
    stored_valid = jnp.broadcast_to(stored_valid, (REQ, DRAFT, CTX))
    causal = jnp.arange(DRAFT, dtype=jnp.int32)[None, :] <= jnp.arange(DRAFT, dtype=jnp.int32)[:, None]
    causal = jnp.broadcast_to(causal[None], (REQ, DRAFT, DRAFT))
    valid = jnp.concatenate([stored_valid, causal], axis=-1)
    attended = mix_heads(rotated, all_keys, all_values, valid)
    projected = jnp.dot(attended, out_weight, preferred_element_type=jnp.float32)
    middle = (flat.astype(jnp.float32) + projected).astype(jnp.bfloat16)
    cross_normed = rms_scale(middle.astype(jnp.float32), cross_norm_gain).astype(jnp.bfloat16)
    cross_queries = jnp.dot(cross_normed, cross_query_weight, preferred_element_type=jnp.float32).astype(jnp.bfloat16)
    cross_queries = cross_queries.reshape(REQ, DRAFT, HEADS, HEAD_DIM)
    normed_queries = rms_scale(cross_queries.astype(jnp.float32), query_gain).astype(jnp.bfloat16)
    image_valid = jnp.arange(IMG, dtype=jnp.int32)[None, None, :] < image_counts[:, None, None]
    image_valid = jnp.broadcast_to(image_valid, (REQ, DRAFT, IMG))
    cross_attended = mix_heads(normed_queries, image_keys.reshape(REQ, IMG, KV_HEADS, HEAD_DIM), image_values.reshape(REQ, IMG, KV_HEADS, HEAD_DIM), image_valid)
    cross_projected = jnp.dot(cross_attended, cross_out_weight, preferred_element_type=jnp.float32)
    layer_out = middle.astype(jnp.float32) + jnp.tanh(cross_gate[0]) * cross_projected
    return layer_out.astype(jnp.bfloat16).reshape(REQ, DRAFT, D)
```

```python
import functools

import jax
import jax.numpy as jnp
from jax import lax
from jax.experimental import pallas as pl
from jax.experimental.pallas import tpu as pltpu
from jax.sharding import PartitionSpec as P

HEADS = 64
KV_HEADS = 8
HEAD_DIM = 128


def rms_scale(values, gain):
    return values * lax.rsqrt(jnp.mean(values * values, axis=-1, keepdims=True) + 1e-05) * gain


def rotate(values, positions):
    half_dim = values.shape[-1] // 2
    freqs = 500000.0 ** (-2.0 * jnp.arange(half_dim, dtype=jnp.float32) / values.shape[-1])
    angles = positions.astype(jnp.float32)[:, :, None, None] * freqs
    cosine = jnp.cos(angles)
    sine = jnp.sin(angles)
    first = values[..., :half_dim]
    second = values[..., half_dim:]
    return jnp.concatenate(
        [first * cosine - second * sine, second * cosine + first * sine], axis=-1
    )


def head_scores(queries, keys, valid):
    requests, drafts = (queries.shape[0], queries.shape[1])
    grouped = queries.reshape(requests, drafts, KV_HEADS, HEADS // KV_HEADS, HEAD_DIM)
    scores = jnp.einsum(
        "rskgd,rtkd->rkgst", grouped, keys, preferred_element_type=jnp.float32
    ) * HEAD_DIM ** (-0.5)
    return jnp.where(valid[:, None, None, :, :], scores, -jnp.inf)


def normalize_scores(scores):
    highest = jnp.max(scores, axis=-1, keepdims=True)
    weights = jnp.exp(scores - highest)
    return (weights / jnp.sum(weights, axis=-1, keepdims=True)).astype(jnp.bfloat16)


def order_by_group(terms):
    rank_count = lax.axis_size("yz")
    group_count = lax.axis_size("gx")
    own_reqs = terms.shape[0] // (rank_count * group_count)
    shaped = terms.reshape(rank_count, group_count, own_reqs, terms.shape[1], terms.shape[2])
    return jnp.swapaxes(shaped, 0, 1).reshape(terms.shape)


def route_features(values):
    return lax.all_to_all(values, "gx", split_axis=2, concat_axis=0, tiled=True)


def project_rows(routed, weights):
    piece = lax.all_gather(routed, "yz", axis=0, tiled=True)
    return jnp.concatenate(
        [
            jnp.einsum("rsd,dc->rsc", piece, matrix, preferred_element_type=jnp.float32)
            for matrix in weights
        ],
        axis=2,
    )


def heads_to_requests(terms):
    summed = lax.psum_scatter(order_by_group(terms), "gx", scatter_dimension=0, tiled=True).astype(
        jnp.bfloat16
    )
    return lax.all_to_all(summed, "yz", split_axis=0, concat_axis=2, tiled=True)


def rows_out(attended, weight):
    blocks = lax.all_to_all(attended, "gx", split_axis=2, concat_axis=0, tiled=True)
    terms = jnp.einsum(
        "rsc,cd->rsd",
        lax.all_gather(blocks, "yz", axis=0, tiled=True),
        weight,
        preferred_element_type=jnp.float32,
    )
    summed = lax.psum_scatter(order_by_group(terms), "gx", scatter_dimension=0, tiled=True)
    return lax.all_to_all(summed, "yz", split_axis=0, concat_axis=2, tiled=True)


def shards_by_collectives(
    hidden,
    cache_lengths,
    image_counts,
    self_keys,
    self_values,
    image_keys,
    image_values,
    norm_gain,
    query_weight,
    kv_weight,
    out_weight,
    cross_norm_gain,
    cross_query_weight,
    query_gain,
    cross_out_weight,
    cross_gate,
):
    own_reqs, drafts = (hidden.shape[0], hidden.shape[1])
    rank_count = lax.axis_size("yz")
    query_cols = query_weight.shape[1]
    normed = rms_scale(hidden.astype(jnp.float32), norm_gain).astype(jnp.bfloat16)
    routed = route_features(normed)
    query_terms = project_rows(routed, (query_weight,))
    kv_terms = jnp.einsum(
        "rsd,dc->rsc",
        lax.all_gather(routed, "yz", axis=0, tiled=True),
        kv_weight,
        preferred_element_type=jnp.float32,
    )
    terms = jnp.concatenate([query_terms, kv_terms], axis=2)
    received = heads_to_requests(terms).reshape(own_reqs, drafts, rank_count, terms.shape[2])
    queries = received[..., :query_cols].reshape(own_reqs, drafts, HEADS, HEAD_DIM)
    fresh = received[..., query_cols:].reshape(own_reqs, drafts, 2, KV_HEADS, HEAD_DIM)
    positions = cache_lengths[:, None] + jnp.arange(drafts, dtype=jnp.int32)[None, :]
    rotated = rotate(queries.astype(jnp.float32), positions).astype(jnp.bfloat16)
    new_keys = rotate(fresh[:, :, 0].astype(jnp.float32), positions).astype(jnp.bfloat16)
    new_values = fresh[:, :, 1]
    stored = self_keys.shape[1]
    stored_keys = self_keys.reshape(own_reqs, stored, KV_HEADS, HEAD_DIM)
    stored_values = self_values.reshape(own_reqs, stored, KV_HEADS, HEAD_DIM)
    stored_valid = jnp.arange(stored, dtype=jnp.int32)[None, None, :] < cache_lengths[:, None, None]
    stored_valid = jnp.broadcast_to(stored_valid, (own_reqs, drafts, stored))
    causal = (
        jnp.arange(drafts, dtype=jnp.int32)[None, :] <= jnp.arange(drafts, dtype=jnp.int32)[:, None]
    )
    causal = causal[None]
    scores = jnp.concatenate(
        [head_scores(rotated, stored_keys, stored_valid), head_scores(rotated, new_keys, causal)],
        axis=-1,
    )
    probs = normalize_scores(scores)
    mixed = jnp.einsum(
        "rkgst,rtkd->rskgd", probs[..., :stored], stored_values, preferred_element_type=jnp.float32
    )
    mixed = mixed + jnp.einsum(
        "rkgst,rtkd->rskgd", probs[..., stored:], new_values, preferred_element_type=jnp.float32
    )
    attended = mixed.astype(jnp.bfloat16).reshape(own_reqs, drafts, HEADS * HEAD_DIM)
    middle = (hidden.astype(jnp.float32) + rows_out(attended, out_weight)).astype(jnp.bfloat16)
    cross_normed = rms_scale(middle.astype(jnp.float32), cross_norm_gain).astype(jnp.bfloat16)
    cross_routed = route_features(cross_normed)
    cross_terms = project_rows(cross_routed, (cross_query_weight,))
    cross_queries = heads_to_requests(cross_terms).reshape(own_reqs, drafts, HEADS, HEAD_DIM)
    normed_queries = rms_scale(cross_queries.astype(jnp.float32), query_gain).astype(jnp.bfloat16)
    slots = image_keys.shape[1]
    image_valid = jnp.arange(slots, dtype=jnp.int32)[None, None, :] < image_counts[:, None, None]
    image_valid = jnp.broadcast_to(image_valid, (own_reqs, drafts, slots))
    cross_probs = normalize_scores(
        head_scores(
            normed_queries, image_keys.reshape(own_reqs, slots, KV_HEADS, HEAD_DIM), image_valid
        )
    )
    cross_mixed = jnp.einsum(
        "rkgst,rtkd->rskgd",
        cross_probs,
        image_values.reshape(own_reqs, slots, KV_HEADS, HEAD_DIM),
        preferred_element_type=jnp.float32,
    )
    cross_attended = cross_mixed.astype(jnp.bfloat16).reshape(own_reqs, drafts, HEADS * HEAD_DIM)
    cross_projected = rows_out(cross_attended, cross_out_weight)
    layer_out = middle.astype(jnp.float32) + jnp.tanh(cross_gate[0]) * cross_projected
    return layer_out.astype(jnp.bfloat16)


LANES = 128
TILE = 16
BF16 = jnp.bfloat16
F32 = jnp.float32


def layer_kernel(
    nz,
    nx,
    drafts,
    lengths_ref,
    counts_ref,
    gate_ref,
    hidden_ref,
    gain_ref,
    cross_gain_ref,
    query_gain_ref,
    cos_ref,
    sin_ref,
    self_keys_ref,
    self_values_ref,
    image_keys_ref,
    image_values_ref,
    wq_ref,
    wkv_ref,
    wo_ref,
    wcq_ref,
    wco_ref,
    out_ref,
    wq,
    wkv,
    wo,
    wcq,
    wco,
    keys,
    values,
    ikeys,
    ivalues,
    hid,
    mid,
    wide,
    lhs,
    rows_out_buf,
    rows_in,
    part_out,
    part_in,
    total,
    tile_f,
    tile_b,
    route_b,
    route_f,
    heads_f,
    heads_b,
    load_sem,
    scat_send,
    scat_recv,
    part_send,
    part_recv,
    route_send,
    route_recv,
):
    n = nz * nx
    j = lax.axis_index("yz")
    i = lax.axis_index("gx")
    me = j * nx + i
    chunks = hid.shape[0] // drafts
    block = chunks // nx
    cols = wo.shape[1] // nx
    per = cols // LANES
    slots = self_keys_ref.shape[0]

    def place(d):
        return {"yz": d // nx, "gx": d % nx}

    loads = [
        (wq_ref, wq),
        (wkv_ref, wkv),
        (self_keys_ref, keys.at[pl.ds(0, slots)]),
        (self_values_ref, values.at[pl.ds(0, slots)]),
        (wo_ref, wo),
        (wcq_ref, wcq),
        (image_keys_ref, ikeys),
        (image_values_ref, ivalues),
        (wco_ref, wco),
    ]
    copies = [pltpu.make_async_copy(a, b, load_sem.at[k]) for k, (a, b) in enumerate(loads)]
    copies[0].start()
    copies[1].start()

    barrier = pltpu.get_barrier_semaphore()

    def greet(k, _):
        pl.semaphore_signal(
            barrier, inc=1, device_id=place((me + k) % n), device_id_type=pl.DeviceIdType.MESH
        )
        return 0

    lax.fori_loop(1, n, greet, 0)

    def norm_rows(rows, gain):
        scaled = []
        for s in range(drafts):
            x = rows[s * chunks : (s + 1) * chunks, :]
            mean = jnp.sum(jnp.sum(x * x, axis=0, keepdims=True), axis=1, keepdims=True) / (
                chunks * LANES
            )
            scaled.append(x * lax.rsqrt(mean + 1e-05) * gain)
        return scaled

    def scatter_copy(stage, k, source, target):
        d = (me + k) % n
        return pltpu.make_async_remote_copy(
            src_ref=rows_out_buf.at[stage, :, pl.ds(pl.multiple_of((source % nx) * block, block), block)],
            dst_ref=rows_in.at[stage, target],
            send_sem=scat_send.at[stage, k],
            recv_sem=scat_recv.at[stage, k],
            device_id=place(d),
            device_id_type=pl.DeviceIdType.MESH,
        )

    def scatter(stage):
        def send(k, _):
            scatter_copy(stage, k, (me + k) % n, me).start()
            return 0

        lax.fori_loop(1, n, send, 0)

    def gather(stage):
        rows = drafts * block
        own = rows_out_buf[stage, :, pl.ds(pl.multiple_of(i * block, block), block), :]
        wide[pl.ds(pl.multiple_of(me * rows, TILE), rows), :] = own.reshape(rows, LANES).astype(F32)

        def take(k, _):
            source = (me - k + n) % n
            scatter_copy(stage, k, me, source).wait_recv()
            got = rows_in[stage, source]
            wide[pl.ds(pl.multiple_of(source * rows, TILE), rows), :] = got.reshape(
                rows, LANES
            ).astype(F32)
            return 0

        lax.fori_loop(1, n, take, 0)
        for s in range(drafts):
            for c in range(block):
                lhs[s * n : (s + 1) * n, c * LANES : (c + 1) * LANES] = wide[
                    pl.ds(s * block + c, n, stride=rows), :
                ].astype(BF16)

    def peer(step, sign):
        half = nx // 2
        flip = nx - 1 - step
        return ((i // 2 + sign * (flip // 2) + half) % half) * 2 + (i % 2 + flip % 2) % 2

    def part_copy(stage, step, width, target):
        return pltpu.make_async_remote_copy(
            src_ref=part_out.at[stage, step, :, pl.ds(0, width)],
            dst_ref=part_in.at[stage, step, :, pl.ds(0, width)],
            send_sem=part_send.at[stage, step],
            recv_sem=part_recv.at[stage, step],
            device_id={"gx": target},
            device_id_type=pl.DeviceIdType.MESH,
        )

    def project(stage, weights):
        width = sum(w.shape[1] // nx for w in weights)

        def piece(target):
            return [
                jnp.dot(
                    lhs[...],
                    w[:, pl.ds(pl.multiple_of(target * (w.shape[1] // nx), LANES), w.shape[1] // nx)],
                    preferred_element_type=F32,
                )
                for w in weights
            ]

        def send(step, _):
            target = peer(step, 1)
            at = 0
            for term in piece(target):
                part_out[stage, step, :, at : at + term.shape[1]] = term
                at += term.shape[1]
            part_copy(stage, step, width, target).start()
            return 0

        lax.fori_loop(0, nx - 1, send, 0)
        at = 0
        for term in piece(i):
            total[:, at : at + term.shape[1]] = term
            at += term.shape[1]
        for step in range(nx - 1):
            part_copy(stage, step, width, peer(step, 1)).wait_recv()
            total[:, :width] += part_in[stage, step, :, :width]
        return width // LANES

    def route_copy(stage, buf_out, buf_in, k, source, target):
        return pltpu.make_async_remote_copy(
            src_ref=buf_out.at[source],
            dst_ref=buf_in.at[target],
            send_sem=route_send.at[stage, k],
            recv_sem=route_recv.at[stage, k],
            device_id=place((me + k) % n),
            device_id_type=pl.DeviceIdType.MESH,
        )

    def route(stage, heads, buf_out, buf_in):
        for s in range(drafts):
            for h in range(heads):
                tile_f[pl.ds(s * heads + h, n, stride=TILE), :] = total[
                    s * n : (s + 1) * n, h * LANES : (h + 1) * LANES
                ]
        buf_out[...] = tile_f[...].reshape(n, TILE, LANES).astype(buf_out.dtype)

        def send(k, _):
            route_copy(stage, buf_out, buf_in, k, (me + k) % n, me).start()
            return 0

        lax.fori_loop(1, n, send, 0)
        buf_in[me] = buf_out[me]

        def take(k, _):
            route_copy(stage, buf_out, buf_in, k, me, (me - k + n) % n).wait_recv()
            return 0

        lax.fori_loop(1, n, take, 0)

    def attend(stage, kref, vref, kv_heads, valid, heads):
        tiles = n // kv_heads
        for k in range(kv_heads):
            q = heads_b[k * tiles * TILE : (k + 1) * tiles * TILE, :]
            lanes = slice(k * LANES, (k + 1) * LANES)
            scores = lax.dot_general(
                q, kref[:, lanes], (((1,), (1,)), ((), ())), preferred_element_type=F32
            ) * LANES ** (-0.5)
            scores = jnp.where(valid, scores, -jnp.inf)
            weights = jnp.exp(scores - jnp.max(scores, axis=-1, keepdims=True))
            probs = (weights / jnp.sum(weights, axis=-1, keepdims=True)).astype(BF16)
            heads_f[k * tiles * TILE : (k + 1) * tiles * TILE, :] = jnp.dot(
                probs, vref[:, lanes], preferred_element_type=F32
            )
        for s in range(drafts):
            for d in range(n):
                at = s * chunks + d * per
                wide[at : at + per, :] = heads_f[
                    d * TILE + s * heads : d * TILE + s * heads + per, :
                ]
        rows_out_buf[stage] = (
            wide[: drafts * chunks, :].reshape(drafts, chunks, LANES).astype(BF16)
        )

    for c in range(chunks):
        hid[pl.ds(c, drafts, stride=chunks), :] = hidden_ref[
            :, c * LANES : (c + 1) * LANES
        ].astype(F32)
    for s, x in enumerate(norm_rows(hid, gain_ref[...])):
        rows_out_buf[0, s] = x.astype(BF16)
    tile_f[...] = jnp.zeros_like(tile_f)
    pl.semaphore_wait(barrier, n - 1)
    scatter(0)
    for copy in copies[2:]:
        copy.start()
    pad = keys.shape[0] - slots
    keys[slots:, :] = jnp.zeros((pad, keys.shape[1]), BF16)
    values[slots:, :] = jnp.zeros((pad, values.shape[1]), BF16)

    gather(0)
    copies[0].wait()
    copies[1].wait()
    heads = project(0, (wq, wkv))
    route(0, heads, tile_b.at[0], route_b.at[0])
    got = route_b[0].reshape(n * TILE, LANES).astype(F32)
    cosine = jnp.concatenate([cos_ref[...]] * n, axis=0)
    sine = jnp.concatenate([sin_ref[...]] * n, axis=0)
    heads_b[...] = (got * cosine + pltpu.roll(got, LANES // 2, 1) * sine).astype(BF16)
    copies[2].wait()
    copies[3].wait()
    kv_heads = n // 2
    for k in range(kv_heads):
        lanes = slice(k * LANES, (k + 1) * LANES)
        keys[slots : slots + TILE, lanes] = heads_b[k * TILE : (k + 1) * TILE, :]
        values[slots : slots + TILE, lanes] = route_b[0, kv_heads + k]
    shape = (n // kv_heads * TILE, keys.shape[0])
    row = lax.broadcasted_iota(jnp.int32, shape, 0) % TILE
    column = lax.broadcasted_iota(jnp.int32, shape, 1)
    valid = column < lengths_ref[0]
    for s in range(drafts):
        valid = valid | ((column == slots + s * heads + per) & (row >= s * heads))
    attend(1, keys, values, kv_heads, valid, heads)
    scatter(1)
    gather(1)
    copies[4].wait()
    heads = project(1, (wo,))
    tile_f[...] = jnp.zeros_like(tile_f)
    route(1, heads, route_f.at[0], route_f.at[1])
    for s in range(drafts):
        for d in range(n):
            at = s * chunks + d * per
            mid[at : at + per, :] = hid[at : at + per, :] + route_f[1, d, s * per : (s + 1) * per, :]
    mid[...] = mid[...].astype(BF16).astype(F32)

    for s, x in enumerate(norm_rows(mid, cross_gain_ref[...])):
        rows_out_buf[2, s] = x.astype(BF16)
    scatter(2)
    gather(2)
    copies[5].wait()
    heads = project(2, (wcq,))
    route(2, heads, tile_b.at[1], route_b.at[1])
    got = route_b[1].reshape(n * TILE, LANES).astype(F32)
    scale = lax.rsqrt(jnp.mean(got * got, axis=-1, keepdims=True) + 1e-05)
    heads_b[...] = (got * scale * query_gain_ref[...]).astype(BF16)
    copies[6].wait()
    copies[7].wait()
    shape = (n // kv_heads * TILE, ikeys.shape[0])
    valid = lax.broadcasted_iota(jnp.int32, shape, 1) < counts_ref[0]
    attend(3, ikeys, ivalues, kv_heads, valid, heads)
    scatter(3)
    gather(3)
    copies[8].wait()
    heads = project(3, (wco,))
    route(3, heads, route_f.at[2], route_f.at[3])
    gate = jnp.tanh(jnp.full((1, LANES), gate_ref[0], F32))
    for s in range(drafts):
        for d in range(n):
            at = s * chunks + d * per
            wide[at : at + per, :] = (
                mid[at : at + per, :] + gate * route_f[3, d, s * per : (s + 1) * per, :]
            )
    for c in range(chunks):
        out_ref[:, c * LANES : (c + 1) * LANES] = wide[
            pl.ds(c, drafts, stride=chunks), :
        ].astype(BF16)

    for stage in range(4):

        def sent(k, _):
            scatter_copy(stage, k, me, me).wait_send()
            out_buf, in_buf = [
                (tile_b.at[0], route_b.at[0]),
                (route_f.at[0], route_f.at[1]),
                (tile_b.at[1], route_b.at[1]),
                (route_f.at[2], route_f.at[3]),
            ][stage]
            route_copy(stage, out_buf, in_buf, k, me, me).wait_send()
            return 0

        lax.fori_loop(1, n, sent, 0)
        width = total.shape[1] if stage == 0 else cols
        for step in range(nx - 1):
            part_copy(stage, step, width, peer(step, 1)).wait_send()


def shards_by_kernel(
    hidden,
    cache_lengths,
    image_counts,
    self_keys,
    self_values,
    image_keys,
    image_values,
    norm_gain,
    query_weight,
    kv_weight,
    out_weight,
    cross_norm_gain,
    cross_query_weight,
    query_gain,
    cross_out_weight,
    cross_gate,
):
    nz, nx = lax.axis_size("yz"), lax.axis_size("gx")
    n = nz * nx
    drafts, model = hidden.shape[1], hidden.shape[2]
    chunks = model // LANES
    cols = query_weight.shape[1] // nx
    width = cols + kv_weight.shape[1] // nx
    per = width // LANES
    position = cache_lengths[0] + jnp.minimum(jnp.arange(TILE, dtype=jnp.int32) // per, drafts - 1)
    half_dim = HEAD_DIM // 2
    freqs = 500000.0 ** (-2.0 * jnp.arange(half_dim, dtype=F32) / HEAD_DIM)
    angles = position.astype(F32)[:, None] * freqs
    cosine, sine = jnp.cos(angles), jnp.sin(angles)
    cosine = jnp.concatenate([cosine, cosine], axis=1)
    sine = jnp.concatenate([-sine, sine], axis=1)
    slots, kv_width = self_keys.shape[1], self_keys.shape[2]
    images = image_keys.shape[1]
    rows = drafts * n
    vmem = pl.BlockSpec(memory_space=pltpu.VMEM)
    smem = pl.BlockSpec(memory_space=pltpu.SMEM)
    away = pl.BlockSpec(memory_space=pl.ANY)
    out = pl.pallas_call(
        functools.partial(layer_kernel, nz, nx, drafts),
        out_shape=jax.ShapeDtypeStruct((drafts, model), BF16),
        in_specs=[smem] * 3 + [vmem] * 6 + [away] * 9,
        out_specs=vmem,
        scratch_shapes=[
            pltpu.VMEM(query_weight.shape, BF16),
            pltpu.VMEM(kv_weight.shape, BF16),
            pltpu.VMEM(out_weight.shape, BF16),
            pltpu.VMEM(cross_query_weight.shape, BF16),
            pltpu.VMEM(cross_out_weight.shape, BF16),
            pltpu.VMEM((slots + LANES, kv_width), BF16),
            pltpu.VMEM((slots + LANES, kv_width), BF16),
            pltpu.VMEM((images, kv_width), BF16),
            pltpu.VMEM((images, kv_width), BF16),
            pltpu.VMEM((drafts * chunks, LANES), F32),
            pltpu.VMEM((drafts * chunks, LANES), F32),
            pltpu.VMEM((n * drafts * (chunks // nx), LANES), F32),
            pltpu.VMEM((rows, model // nx), BF16),
            pltpu.VMEM((4, drafts, chunks, LANES), BF16),
            pltpu.VMEM((4, n, drafts, chunks // nx, LANES), BF16),
            pltpu.VMEM((4, nx - 1, rows, width), F32),
            pltpu.VMEM((4, nx - 1, rows, width), F32),
            pltpu.VMEM((rows, width), F32),
            pltpu.VMEM((n * TILE, LANES), F32),
            pltpu.VMEM((2, n, TILE, LANES), BF16),
            pltpu.VMEM((2, n, TILE, LANES), BF16),
            pltpu.VMEM((4, n, TILE, LANES), F32),
            pltpu.VMEM((n * TILE, LANES), F32),
            pltpu.VMEM((n * TILE, LANES), BF16),
            pltpu.SemaphoreType.DMA((9,)),
            pltpu.SemaphoreType.DMA((4, n)),
            pltpu.SemaphoreType.DMA((4, n)),
            pltpu.SemaphoreType.DMA((4, nx - 1)),
            pltpu.SemaphoreType.DMA((4, nx - 1)),
            pltpu.SemaphoreType.DMA((4, n)),
            pltpu.SemaphoreType.DMA((4, n)),
        ],
        compiler_params=pltpu.CompilerParams(
            collective_id=0, has_side_effects=True, vmem_limit_bytes=56 * 2**20
        ),
        cost_estimate=pl.CostEstimate(
            flops=2 * rows * query_weight.shape[0] * (4 * query_weight.shape[1] + kv_weight.shape[1]),
            bytes_accessed=2 * query_weight.shape[0] * (4 * query_weight.shape[1] + kv_weight.shape[1]),
            transcendentals=0,
        ),
    )(
        cache_lengths,
        image_counts,
        cross_gate,
        hidden.reshape(drafts, model),
        norm_gain.reshape(chunks, LANES),
        cross_norm_gain.reshape(chunks, LANES),
        query_gain.reshape(1, HEAD_DIM),
        cosine,
        sine,
        self_keys.reshape(slots, kv_width),
        self_values.reshape(slots, kv_width),
        image_keys.reshape(images, kv_width),
        image_values.reshape(images, kv_width),
        query_weight,
        kv_weight,
        out_weight,
        cross_query_weight,
        cross_out_weight,
    )
    return out.reshape(hidden.shape)


def fits_kernel(hidden, kv_weight, query_weight):
    nx = lax.axis_size("gx")
    n = lax.axis_size("yz") * nx
    per = query_weight.shape[1] // nx // HEAD_DIM
    return (
        hidden.shape[0] == 1
        and n == 2 * KV_HEADS
        and nx % 2 == 0
        and query_weight.shape[1] == nx * per * HEAD_DIM
        and per * n == HEADS
        and kv_weight.shape[1] == nx * HEAD_DIM
        and hidden.shape[1] * (per + 1) <= TILE
        and query_weight.shape[0] % (TILE * LANES) == 0
    )


def shards(hidden, *rest):
    if fits_kernel(hidden, rest[8], rest[7]):
        return shards_by_kernel(hidden, *rest)
    return shards_by_collectives(hidden, *rest)


def solution(mesh):
    placed = (
        P(("grp", "yz", "gx"), None, None),
        P(("grp", "yz", "gx")),
        P(("grp", "yz", "gx")),
        P(("grp", "yz", "gx"), None, None),
        P(("grp", "yz", "gx"), None, None),
        P(("grp", "yz", "gx"), None, None),
        P(("grp", "yz", "gx"), None, None),
        P(),
        P("gx", "yz"),
        P("gx", "yz"),
        P("gx", "yz"),
        P(),
        P("gx", "yz"),
        P(),
        P("gx", "yz"),
        P(),
    )
    return jax.shard_map(
        shards,
        mesh=mesh,
        in_specs=placed,
        out_specs=P(("grp", "yz", "gx"), None, None),
        check_vma=False,
    )
```

```python
import functools

import jax
import jax.numpy as jnp
from jax import lax
from jax.experimental import pallas as pl
from jax.experimental.pallas import tpu as pltpu
from jax.sharding import PartitionSpec as P

HEADS = 64
KV_HEADS = 8
HEAD_DIM = 128


def rms_scale(values, gain):
    return values * lax.rsqrt(jnp.mean(values * values, axis=-1, keepdims=True) + 1e-05) * gain


def rotate(values, positions):
    half_dim = values.shape[-1] // 2
    freqs = 500000.0 ** (-2.0 * jnp.arange(half_dim, dtype=jnp.float32) / values.shape[-1])
    angles = positions.astype(jnp.float32)[:, :, None, None] * freqs
    cosine = jnp.cos(angles)
    sine = jnp.sin(angles)
    first = values[..., :half_dim]
    second = values[..., half_dim:]
    return jnp.concatenate(
        [first * cosine - second * sine, second * cosine + first * sine], axis=-1
    )


def head_scores(queries, keys, valid):
    requests, drafts = (queries.shape[0], queries.shape[1])
    grouped = queries.reshape(requests, drafts, KV_HEADS, HEADS // KV_HEADS, HEAD_DIM)
    scores = jnp.einsum(
        "rskgd,rtkd->rkgst", grouped, keys, preferred_element_type=jnp.float32
    ) * HEAD_DIM ** (-0.5)
    return jnp.where(valid[:, None, None, :, :], scores, -jnp.inf)


def normalize_scores(scores):
    highest = jnp.max(scores, axis=-1, keepdims=True)
    weights = jnp.exp(scores - highest)
    return (weights / jnp.sum(weights, axis=-1, keepdims=True)).astype(jnp.bfloat16)


def order_by_group(terms):
    rank_count = lax.axis_size("yz")
    group_count = lax.axis_size("gx")
    own_reqs = terms.shape[0] // (rank_count * group_count)
    shaped = terms.reshape(rank_count, group_count, own_reqs, terms.shape[1], terms.shape[2])
    return jnp.swapaxes(shaped, 0, 1).reshape(terms.shape)


def route_features(values):
    return lax.all_to_all(values, "gx", split_axis=2, concat_axis=0, tiled=True)


def project_rows(routed, weights):
    piece = lax.all_gather(routed, "yz", axis=0, tiled=True)
    return jnp.concatenate(
        [
            jnp.einsum("rsd,dc->rsc", piece, matrix, preferred_element_type=jnp.float32)
            for matrix in weights
        ],
        axis=2,
    )


def heads_to_requests(terms):
    summed = lax.psum_scatter(order_by_group(terms), "gx", scatter_dimension=0, tiled=True).astype(
        jnp.bfloat16
    )
    return lax.all_to_all(summed, "yz", split_axis=0, concat_axis=2, tiled=True)


def rows_out(attended, weight):
    blocks = lax.all_to_all(attended, "gx", split_axis=2, concat_axis=0, tiled=True)
    terms = jnp.einsum(
        "rsc,cd->rsd",
        lax.all_gather(blocks, "yz", axis=0, tiled=True),
        weight,
        preferred_element_type=jnp.float32,
    )
    summed = lax.psum_scatter(order_by_group(terms), "gx", scatter_dimension=0, tiled=True)
    return lax.all_to_all(summed, "yz", split_axis=0, concat_axis=2, tiled=True)


def shards_by_collectives(
    hidden,
    cache_lengths,
    image_counts,
    self_keys,
    self_values,
    image_keys,
    image_values,
    norm_gain,
    query_weight,
    kv_weight,
    out_weight,
    cross_norm_gain,
    cross_query_weight,
    query_gain,
    cross_out_weight,
    cross_gate,
):
    own_reqs, drafts = (hidden.shape[0], hidden.shape[1])
    rank_count = lax.axis_size("yz")
    query_cols = query_weight.shape[1]
    normed = rms_scale(hidden.astype(jnp.float32), norm_gain).astype(jnp.bfloat16)
    routed = route_features(normed)
    query_terms = project_rows(routed, (query_weight,))
    kv_terms = jnp.einsum(
        "rsd,dc->rsc",
        lax.all_gather(routed, "yz", axis=0, tiled=True),
        kv_weight,
        preferred_element_type=jnp.float32,
    )
    terms = jnp.concatenate([query_terms, kv_terms], axis=2)
    received = heads_to_requests(terms).reshape(own_reqs, drafts, rank_count, terms.shape[2])
    queries = received[..., :query_cols].reshape(own_reqs, drafts, HEADS, HEAD_DIM)
    fresh = received[..., query_cols:].reshape(own_reqs, drafts, 2, KV_HEADS, HEAD_DIM)
    positions = cache_lengths[:, None] + jnp.arange(drafts, dtype=jnp.int32)[None, :]
    rotated = rotate(queries.astype(jnp.float32), positions).astype(jnp.bfloat16)
    new_keys = rotate(fresh[:, :, 0].astype(jnp.float32), positions).astype(jnp.bfloat16)
    new_values = fresh[:, :, 1]
    stored = self_keys.shape[1]
    stored_keys = self_keys.reshape(own_reqs, stored, KV_HEADS, HEAD_DIM)
    stored_values = self_values.reshape(own_reqs, stored, KV_HEADS, HEAD_DIM)
    stored_valid = jnp.arange(stored, dtype=jnp.int32)[None, None, :] < cache_lengths[:, None, None]
    stored_valid = jnp.broadcast_to(stored_valid, (own_reqs, drafts, stored))
    causal = (
        jnp.arange(drafts, dtype=jnp.int32)[None, :] <= jnp.arange(drafts, dtype=jnp.int32)[:, None]
    )
    causal = causal[None]
    scores = jnp.concatenate(
        [head_scores(rotated, stored_keys, stored_valid), head_scores(rotated, new_keys, causal)],
        axis=-1,
    )
    probs = normalize_scores(scores)
    mixed = jnp.einsum(
        "rkgst,rtkd->rskgd", probs[..., :stored], stored_values, preferred_element_type=jnp.float32
    )
    mixed = mixed + jnp.einsum(
        "rkgst,rtkd->rskgd", probs[..., stored:], new_values, preferred_element_type=jnp.float32
    )
    attended = mixed.astype(jnp.bfloat16).reshape(own_reqs, drafts, HEADS * HEAD_DIM)
    middle = (hidden.astype(jnp.float32) + rows_out(attended, out_weight)).astype(jnp.bfloat16)
    cross_normed = rms_scale(middle.astype(jnp.float32), cross_norm_gain).astype(jnp.bfloat16)
    cross_routed = route_features(cross_normed)
    cross_terms = project_rows(cross_routed, (cross_query_weight,))
    cross_queries = heads_to_requests(cross_terms).reshape(own_reqs, drafts, HEADS, HEAD_DIM)
    normed_queries = rms_scale(cross_queries.astype(jnp.float32), query_gain).astype(jnp.bfloat16)
    slots = image_keys.shape[1]
    image_valid = jnp.arange(slots, dtype=jnp.int32)[None, None, :] < image_counts[:, None, None]
    image_valid = jnp.broadcast_to(image_valid, (own_reqs, drafts, slots))
    cross_probs = normalize_scores(
        head_scores(
            normed_queries, image_keys.reshape(own_reqs, slots, KV_HEADS, HEAD_DIM), image_valid
        )
    )
    cross_mixed = jnp.einsum(
        "rkgst,rtkd->rskgd",
        cross_probs,
        image_values.reshape(own_reqs, slots, KV_HEADS, HEAD_DIM),
        preferred_element_type=jnp.float32,
    )
    cross_attended = cross_mixed.astype(jnp.bfloat16).reshape(own_reqs, drafts, HEADS * HEAD_DIM)
    cross_projected = rows_out(cross_attended, cross_out_weight)
    layer_out = middle.astype(jnp.float32) + jnp.tanh(cross_gate[0]) * cross_projected
    return layer_out.astype(jnp.bfloat16)


LANES = 128
TILE = 16
BF16 = jnp.bfloat16
F32 = jnp.float32


def layer_kernel(
    nz,
    nx,
    drafts,
    lengths_ref,
    counts_ref,
    gate_ref,
    hidden_ref,
    gain_ref,
    cross_gain_ref,
    query_gain_ref,
    cos_ref,
    sin_ref,
    self_keys_ref,
    self_values_ref,
    image_keys_ref,
    image_values_ref,
    wq_ref,
    wkv_ref,
    wo_ref,
    wcq_ref,
    wco_ref,
    out_ref,
    wq,
    wkv,
    wo,
    wcq,
    wco,
    keys,
    values,
    ikeys,
    ivalues,
    hid,
    mid,
    wide,
    lhs,
    rows_out_buf,
    rows_in,
    part_out,
    part_in,
    total,
    tile_f,
    tile_b,
    route_b,
    heads_f,
    heads_b,
    load_sem,
    scat_send,
    scat_recv,
    part_send,
    part_recv,
    route_send,
    route_recv,
):
    n = nz * nx
    j = lax.axis_index("yz")
    i = lax.axis_index("gx")
    me = j * nx + i
    chunks = hid.shape[0] // drafts
    block = chunks // nx
    cols = wo.shape[1] // nx
    per = cols // LANES
    slots = self_keys_ref.shape[0]

    def place(d):
        return {"yz": d // nx, "gx": d % nx}

    loads = [
        (wq_ref, wq),
        (wkv_ref, wkv),
        (self_keys_ref, keys.at[pl.ds(0, slots)]),
        (self_values_ref, values.at[pl.ds(0, slots)]),
        (wo_ref, wo),
        (wcq_ref, wcq),
        (image_keys_ref, ikeys),
        (image_values_ref, ivalues),
        (wco_ref, wco),
    ]
    copies = [pltpu.make_async_copy(a, b, load_sem.at[k]) for k, (a, b) in enumerate(loads)]
    copies[0].start()
    copies[1].start()

    barrier = pltpu.get_barrier_semaphore()

    def greet(k, _):
        pl.semaphore_signal(
            barrier, inc=1, device_id=place((me + k) % n), device_id_type=pl.DeviceIdType.MESH
        )
        return 0

    lax.fori_loop(1, n, greet, 0, unroll=True)

    def norm_rows(rows, gain):
        scaled = []
        for s in range(drafts):
            x = rows[s * chunks : (s + 1) * chunks, :]
            mean = jnp.sum(jnp.sum(x * x, axis=0, keepdims=True), axis=1, keepdims=True) / (
                chunks * LANES
            )
            scaled.append(x * lax.rsqrt(mean + 1e-05) * gain)
        return scaled

    def far_first(k):
        return (k + n // 2 - 2) % (n - 1) + 1

    def scatter_copy(stage, k, source, target):
        d = (me + k) % n
        return pltpu.make_async_remote_copy(
            src_ref=rows_out_buf.at[stage, :, pl.ds(pl.multiple_of((source % nx) * block, block), block)],
            dst_ref=rows_in.at[stage, target],
            send_sem=scat_send.at[stage, k],
            recv_sem=scat_recv.at[stage, k],
            device_id=place(d),
            device_id_type=pl.DeviceIdType.MESH,
        )

    def scatter(stage):
        def send(k, _):
            k = far_first(k)
            scatter_copy(stage, k, (me + k) % n, me).start()
            return 0

        lax.fori_loop(1, n, send, 0, unroll=True)

    def gather(stage):
        rows = drafts * block
        own = rows_out_buf[stage, :, pl.ds(pl.multiple_of(i * block, block), block), :]
        wide[pl.ds(pl.multiple_of(me * rows, TILE), rows), :] = own.reshape(rows, LANES).astype(F32)

        def take(k, _):
            source = (me - k + n) % n
            scatter_copy(stage, k, me, source).wait_recv()
            got = rows_in[stage, source]
            wide[pl.ds(pl.multiple_of(source * rows, TILE), rows), :] = got.reshape(
                rows, LANES
            ).astype(F32)
            return 0

        lax.fori_loop(1, n, take, 0, unroll=True)
        for s in range(drafts):
            for c in range(block):
                lhs[s * n : (s + 1) * n, c * LANES : (c + 1) * LANES] = wide[
                    pl.ds(s * block + c, n, stride=rows), :
                ].astype(BF16)

    across_chip = (1 - i // 2) * 2
    same_chip = i // 2 * 2
    other_core = 1 - i % 2
    peers = (same_chip + other_core, across_chip + i % 2, same_chip + other_core)

    def part_copy(stage, step, width, target):
        return pltpu.make_async_remote_copy(
            src_ref=part_out.at[stage, step, :, pl.ds(0, width)],
            dst_ref=part_in.at[stage, step, :, pl.ds(0, width)],
            send_sem=part_send.at[stage, step],
            recv_sem=part_recv.at[stage, step],
            device_id={"gx": target},
            device_id_type=pl.DeviceIdType.MESH,
        )

    def project(stage, weights):
        width = sum(w.shape[1] // nx for w in weights)

        def piece(target):
            return [
                jnp.dot(
                    lhs[...],
                    w[:, pl.ds(pl.multiple_of(target * (w.shape[1] // nx), LANES), w.shape[1] // nx)],
                    preferred_element_type=F32,
                )
                for w in weights
            ]

        def store(ref, target):
            at = 0
            for term in piece(target):
                ref[:, at : at + term.shape[1]] = term
                at += term.shape[1]

        def link(step):
            return part_copy(stage, step, width, peers[step])

        store(part_out.at[stage, 0], across_chip + other_core)
        link(0).start()
        store(part_out.at[stage, 1], across_chip + i % 2)
        link(0).wait_recv()
        part_out[stage, 1, :, :width] += part_in[stage, 0, :, :width]
        link(1).start()
        store(part_out.at[stage, 2], peers[2])
        link(2).start()
        store(total, i)
        link(2).wait_recv()
        total[:, :width] += part_in[stage, 2, :, :width]
        link(1).wait_recv()
        total[:, :width] += part_in[stage, 1, :, :width]
        return width // LANES

    def route_copy(stage, buf_out, buf_in, k, source, target):
        return pltpu.make_async_remote_copy(
            src_ref=buf_out.at[source],
            dst_ref=buf_in.at[target],
            send_sem=route_send.at[stage, k],
            recv_sem=route_recv.at[stage, k],
            device_id=place((me + k) % n),
            device_id_type=pl.DeviceIdType.MESH,
        )

    def route(stage, heads, finish=lambda rows: rows):
        buf_out, buf_in = tile_b.at[stage], route_b.at[stage]
        for s in range(drafts):
            for h in range(heads):
                tile_f[pl.ds(s * heads + h, n, stride=TILE), :] = total[
                    s * n : (s + 1) * n, h * LANES : (h + 1) * LANES
                ]
        buf_out[...] = finish(tile_f[...]).reshape(n, TILE, LANES).astype(BF16)
        exchange(stage)
        collect(stage)

    def exchange(stage):
        buf_out, buf_in = tile_b.at[stage], route_b.at[stage]

        def send(k, _):
            k = far_first(k)
            route_copy(stage, buf_out, buf_in, k, (me + k) % n, me).start()
            return 0

        lax.fori_loop(1, n, send, 0, unroll=True)
        buf_in[me] = buf_out[me]

    def collect(stage):
        buf_out, buf_in = tile_b.at[stage], route_b.at[stage]

        def take(k, _):
            route_copy(stage, buf_out, buf_in, k, me, (me - k + n) % n).wait_recv()
            return 0

        lax.fori_loop(1, n, take, 0, unroll=True)

    def attend(stage, kref, vref, kv_heads, valid, heads):
        tiles = n // kv_heads
        height = tiles * TILE
        scores = []
        for k in range(kv_heads):
            part = lax.dot_general(
                heads_b[k * height : (k + 1) * height, :],
                kref[:, k * LANES : (k + 1) * LANES],
                (((1,), (1,)), ((), ())),
                preferred_element_type=F32,
            )
            scores.append(jnp.where(valid, part * LANES ** (-0.5), -jnp.inf))
        scores = jnp.concatenate(scores, axis=0)
        weights = jnp.exp(scores - jnp.max(scores, axis=-1, keepdims=True))
        probs = (weights / jnp.sum(weights, axis=-1, keepdims=True)).astype(BF16)
        for k in range(kv_heads):
            heads_f[k * height : (k + 1) * height, :] = jnp.dot(
                probs[k * height : (k + 1) * height, :],
                vref[:, k * LANES : (k + 1) * LANES],
                preferred_element_type=F32,
            )
        for s in range(drafts):
            for d in range(n):
                at = s * chunks + d * per
                wide[at : at + per, :] = heads_f[
                    d * TILE + s * heads : d * TILE + s * heads + per, :
                ]
        rows_out_buf[stage] = (
            wide[: drafts * chunks, :].reshape(drafts, chunks, LANES).astype(BF16)
        )

    def from_tiles(stage, ref):
        heads_f[...] = route_b[stage].reshape(n * TILE, LANES).astype(F32)
        for s in range(drafts):
            for d in range(n):
                ref[s * chunks + d * per : s * chunks + (d + 1) * per, :] = heads_f[
                    d * TILE + s * per : d * TILE + (s + 1) * per, :
                ]

    for c in range(chunks):
        hid[pl.ds(c, drafts, stride=chunks), :] = hidden_ref[
            :, c * LANES : (c + 1) * LANES
        ].astype(F32)
    for s, x in enumerate(norm_rows(hid, gain_ref[...])):
        rows_out_buf[0, s] = x.astype(BF16)
    tile_f[...] = jnp.zeros_like(tile_f)
    pl.semaphore_wait(barrier, n - 1)
    scatter(0)
    for s in range(drafts):
        for d in range(n):
            tile_f[d * TILE + s * per : d * TILE + (s + 1) * per, :] = hid[
                s * chunks + d * per : s * chunks + (d + 1) * per, :
            ]
    tile_b[4] = tile_f[...].reshape(n, TILE, LANES).astype(BF16)
    exchange(4)
    tile_f[...] = jnp.zeros_like(tile_f)
    for copy in copies[2:]:
        copy.start()
    pad = keys.shape[0] - slots
    keys[slots:, :] = jnp.zeros((pad, keys.shape[1]), BF16)
    values[slots:, :] = jnp.zeros((pad, values.shape[1]), BF16)

    gather(0)
    copies[0].wait()
    copies[1].wait()
    heads = project(0, (wq, wkv))
    route(0, heads)
    got = route_b[0].reshape(n * TILE, LANES).astype(F32)
    cosine = jnp.concatenate([cos_ref[...]] * n, axis=0)
    sine = jnp.concatenate([sin_ref[...]] * n, axis=0)
    heads_b[...] = (got * cosine + pltpu.roll(got, LANES // 2, 1) * sine).astype(BF16)
    copies[2].wait()
    copies[3].wait()
    kv_heads = n // 2
    for k in range(kv_heads):
        lanes = slice(k * LANES, (k + 1) * LANES)
        keys[slots : slots + TILE, lanes] = heads_b[k * TILE : (k + 1) * TILE, :]
        values[slots : slots + TILE, lanes] = route_b[0, kv_heads + k]
    shape = (n // kv_heads * TILE, keys.shape[0])
    row = lax.broadcasted_iota(jnp.int32, shape, 0) % TILE
    column = lax.broadcasted_iota(jnp.int32, shape, 1)
    valid = column < lengths_ref[0]
    for s in range(drafts):
        valid = valid | ((column == slots + s * heads + per) & (row >= s * heads))
    attend(1, keys, values, kv_heads, valid, heads)
    scatter(1)
    gather(1)
    copies[4].wait()
    heads = project(1, (wo,))
    tile_f[...] = jnp.zeros_like(tile_f)
    collect(4)
    route(
        1, heads, lambda rows: rows + route_b[4].reshape(n * TILE, LANES).astype(F32)
    )
    from_tiles(1, mid)

    for s, x in enumerate(norm_rows(mid, cross_gain_ref[...])):
        rows_out_buf[2, s] = x.astype(BF16)
    scatter(2)
    gather(2)
    copies[5].wait()
    heads = project(2, (wcq,))
    route(2, heads)
    got = route_b[2].reshape(n * TILE, LANES).astype(F32)
    scale = lax.rsqrt(jnp.mean(got * got, axis=-1, keepdims=True) + 1e-05)
    heads_b[...] = (got * scale * query_gain_ref[...]).astype(BF16)
    copies[6].wait()
    copies[7].wait()
    shape = (n // kv_heads * TILE, ikeys.shape[0])
    valid = lax.broadcasted_iota(jnp.int32, shape, 1) < counts_ref[0]
    attend(3, ikeys, ivalues, kv_heads, valid, heads)
    scatter(3)
    gather(3)
    copies[8].wait()
    heads = project(3, (wco,))
    gate = jnp.tanh(jnp.full((1, LANES), gate_ref[0], F32))
    route(
        3,
        heads,
        lambda rows: tile_b[1].reshape(n * TILE, LANES).astype(F32) + gate * rows,
    )
    from_tiles(3, mid)
    for c in range(chunks):
        out_ref[:, c * LANES : (c + 1) * LANES] = mid[
            pl.ds(c, drafts, stride=chunks), :
        ].astype(BF16)

    def gone(k, _):
        route_copy(4, tile_b.at[4], route_b.at[4], k, me, me).wait_send()
        return 0

    lax.fori_loop(1, n, gone, 0)
    for stage in range(4):

        def sent(k, _):
            scatter_copy(stage, k, me, me).wait_send()
            route_copy(stage, tile_b.at[stage], route_b.at[stage], k, me, me).wait_send()
            return 0

        lax.fori_loop(1, n, sent, 0)
        width = total.shape[1] if stage == 0 else cols
        for step in range(nx - 1):
            part_copy(stage, step, width, peers[step]).wait_send()


def shards_by_kernel(
    hidden,
    cache_lengths,
    image_counts,
    self_keys,
    self_values,
    image_keys,
    image_values,
    norm_gain,
    query_weight,
    kv_weight,
    out_weight,
    cross_norm_gain,
    cross_query_weight,
    query_gain,
    cross_out_weight,
    cross_gate,
):
    nz, nx = lax.axis_size("yz"), lax.axis_size("gx")
    n = nz * nx
    drafts, model = hidden.shape[1], hidden.shape[2]
    chunks = model // LANES
    cols = query_weight.shape[1] // nx
    width = cols + kv_weight.shape[1] // nx
    per = width // LANES
    position = cache_lengths[0] + jnp.minimum(jnp.arange(TILE, dtype=jnp.int32) // per, drafts - 1)
    half_dim = HEAD_DIM // 2
    freqs = 500000.0 ** (-2.0 * jnp.arange(half_dim, dtype=F32) / HEAD_DIM)
    angles = position.astype(F32)[:, None] * freqs
    cosine, sine = jnp.cos(angles), jnp.sin(angles)
    cosine = jnp.concatenate([cosine, cosine], axis=1)
    sine = jnp.concatenate([-sine, sine], axis=1)
    slots, kv_width = self_keys.shape[1], self_keys.shape[2]
    images = image_keys.shape[1]
    rows = drafts * n
    vmem = pl.BlockSpec(memory_space=pltpu.VMEM)
    smem = pl.BlockSpec(memory_space=pltpu.SMEM)
    away = pl.BlockSpec(memory_space=pl.ANY)
    out = pl.pallas_call(
        functools.partial(layer_kernel, nz, nx, drafts),
        out_shape=jax.ShapeDtypeStruct((drafts, model), BF16),
        in_specs=[smem] * 3 + [vmem] * 6 + [away] * 9,
        out_specs=vmem,
        scratch_shapes=[
            pltpu.VMEM(query_weight.shape, BF16),
            pltpu.VMEM(kv_weight.shape, BF16),
            pltpu.VMEM(out_weight.shape, BF16),
            pltpu.VMEM(cross_query_weight.shape, BF16),
            pltpu.VMEM(cross_out_weight.shape, BF16),
            pltpu.VMEM((slots + LANES, kv_width), BF16),
            pltpu.VMEM((slots + LANES, kv_width), BF16),
            pltpu.VMEM((images, kv_width), BF16),
            pltpu.VMEM((images, kv_width), BF16),
            pltpu.VMEM((drafts * chunks, LANES), F32),
            pltpu.VMEM((drafts * chunks, LANES), F32),
            pltpu.VMEM((n * drafts * (chunks // nx), LANES), F32),
            pltpu.VMEM((rows, model // nx), BF16),
            pltpu.VMEM((4, drafts, chunks, LANES), BF16),
            pltpu.VMEM((4, n, drafts, chunks // nx, LANES), BF16),
            pltpu.VMEM((4, nx - 1, rows, width), F32),
            pltpu.VMEM((4, nx - 1, rows, width), F32),
            pltpu.VMEM((rows, width), F32),
            pltpu.VMEM((n * TILE, LANES), F32),
            pltpu.VMEM((5, n, TILE, LANES), BF16),
            pltpu.VMEM((5, n, TILE, LANES), BF16),
            pltpu.VMEM((n * TILE, LANES), F32),
            pltpu.VMEM((n * TILE, LANES), BF16),
            pltpu.SemaphoreType.DMA((9,)),
            pltpu.SemaphoreType.DMA((4, n)),
            pltpu.SemaphoreType.DMA((4, n)),
            pltpu.SemaphoreType.DMA((4, nx - 1)),
            pltpu.SemaphoreType.DMA((4, nx - 1)),
            pltpu.SemaphoreType.DMA((5, n)),
            pltpu.SemaphoreType.DMA((5, n)),
        ],
        compiler_params=pltpu.CompilerParams(
            collective_id=0, has_side_effects=True, vmem_limit_bytes=56 * 2**20
        ),
        cost_estimate=pl.CostEstimate(
            flops=2 * rows * query_weight.shape[0] * (4 * query_weight.shape[1] + kv_weight.shape[1]),
            bytes_accessed=2 * query_weight.shape[0] * (4 * query_weight.shape[1] + kv_weight.shape[1]),
            transcendentals=0,
        ),
    )(
        cache_lengths,
        image_counts,
        cross_gate,
        hidden.reshape(drafts, model),
        norm_gain.reshape(chunks, LANES),
        cross_norm_gain.reshape(chunks, LANES),
        query_gain.reshape(1, HEAD_DIM),
        cosine,
        sine,
        self_keys.reshape(slots, kv_width),
        self_values.reshape(slots, kv_width),
        image_keys.reshape(images, kv_width),
        image_values.reshape(images, kv_width),
        query_weight,
        kv_weight,
        out_weight,
        cross_query_weight,
        cross_out_weight,
    )
    return out.reshape(hidden.shape)


def fits_kernel(hidden, kv_weight, query_weight):
    nx = lax.axis_size("gx")
    n = lax.axis_size("yz") * nx
    per = query_weight.shape[1] // nx // HEAD_DIM
    return (
        hidden.shape[0] == 1
        and n == 2 * KV_HEADS
        and nx == 4
        and query_weight.shape[1] == nx * per * HEAD_DIM
        and per * n == HEADS
        and kv_weight.shape[1] == nx * HEAD_DIM
        and hidden.shape[1] * (per + 1) <= TILE
        and query_weight.shape[0] % (TILE * LANES) == 0
    )


def shards(hidden, *rest):
    if fits_kernel(hidden, rest[8], rest[7]):
        return shards_by_kernel(hidden, *rest)
    return shards_by_collectives(hidden, *rest)


def solution(mesh):
    placed = (
        P(("grp", "yz", "gx"), None, None),
        P(("grp", "yz", "gx")),
        P(("grp", "yz", "gx")),
        P(("grp", "yz", "gx"), None, None),
        P(("grp", "yz", "gx"), None, None),
        P(("grp", "yz", "gx"), None, None),
        P(("grp", "yz", "gx"), None, None),
        P(),
        P("gx", "yz"),
        P("gx", "yz"),
        P("gx", "yz"),
        P(),
        P("gx", "yz"),
        P(),
        P("gx", "yz"),
        P(),
    )
    return jax.shard_map(
        shards,
        mesh=mesh,
        in_specs=placed,
        out_specs=P(("grp", "yz", "gx"), None, None),
        check_vma=False,
    )
```

```python
import functools

import jax
import jax.numpy as jnp
from jax import lax
from jax.experimental import pallas as pl
from jax.experimental.pallas import tpu as pltpu
from jax.sharding import PartitionSpec as P

HEADS = 64
KV_HEADS = 8
HEAD_DIM = 128


def rms_scale(values, gain):
    return values * lax.rsqrt(jnp.mean(values * values, axis=-1, keepdims=True) + 1e-05) * gain


def rotate(values, positions):
    half_dim = values.shape[-1] // 2
    freqs = 500000.0 ** (-2.0 * jnp.arange(half_dim, dtype=jnp.float32) / values.shape[-1])
    angles = positions.astype(jnp.float32)[:, :, None, None] * freqs
    cosine = jnp.cos(angles)
    sine = jnp.sin(angles)
    first = values[..., :half_dim]
    second = values[..., half_dim:]
    return jnp.concatenate(
        [first * cosine - second * sine, second * cosine + first * sine], axis=-1
    )


def head_scores(queries, keys, valid):
    requests, drafts = (queries.shape[0], queries.shape[1])
    grouped = queries.reshape(requests, drafts, KV_HEADS, HEADS // KV_HEADS, HEAD_DIM)
    scores = jnp.einsum(
        "rskgd,rtkd->rkgst", grouped, keys, preferred_element_type=jnp.float32
    ) * HEAD_DIM ** (-0.5)
    return jnp.where(valid[:, None, None, :, :], scores, -jnp.inf)


def normalize_scores(scores):
    highest = jnp.max(scores, axis=-1, keepdims=True)
    weights = jnp.exp(scores - highest)
    return (weights / jnp.sum(weights, axis=-1, keepdims=True)).astype(jnp.bfloat16)


def order_by_group(terms):
    rank_count = lax.axis_size("yz")
    group_count = lax.axis_size("gx")
    own_reqs = terms.shape[0] // (rank_count * group_count)
    shaped = terms.reshape(rank_count, group_count, own_reqs, terms.shape[1], terms.shape[2])
    return jnp.swapaxes(shaped, 0, 1).reshape(terms.shape)


def route_features(values):
    return lax.all_to_all(values, "gx", split_axis=2, concat_axis=0, tiled=True)


def project_rows(routed, weights):
    piece = lax.all_gather(routed, "yz", axis=0, tiled=True)
    return jnp.concatenate(
        [
            jnp.einsum("rsd,dc->rsc", piece, matrix, preferred_element_type=jnp.float32)
            for matrix in weights
        ],
        axis=2,
    )


def heads_to_requests(terms):
    summed = lax.psum_scatter(order_by_group(terms), "gx", scatter_dimension=0, tiled=True).astype(
        jnp.bfloat16
    )
    return lax.all_to_all(summed, "yz", split_axis=0, concat_axis=2, tiled=True)


def rows_out(attended, weight):
    blocks = lax.all_to_all(attended, "gx", split_axis=2, concat_axis=0, tiled=True)
    terms = jnp.einsum(
        "rsc,cd->rsd",
        lax.all_gather(blocks, "yz", axis=0, tiled=True),
        weight,
        preferred_element_type=jnp.float32,
    )
    summed = lax.psum_scatter(order_by_group(terms), "gx", scatter_dimension=0, tiled=True)
    return lax.all_to_all(summed, "yz", split_axis=0, concat_axis=2, tiled=True)


def shards_by_collectives(
    hidden,
    cache_lengths,
    image_counts,
    self_keys,
    self_values,
    image_keys,
    image_values,
    norm_gain,
    query_weight,
    kv_weight,
    out_weight,
    cross_norm_gain,
    cross_query_weight,
    query_gain,
    cross_out_weight,
    cross_gate,
):
    own_reqs, drafts = (hidden.shape[0], hidden.shape[1])
    rank_count = lax.axis_size("yz")
    query_cols = query_weight.shape[1]
    normed = rms_scale(hidden.astype(jnp.float32), norm_gain).astype(jnp.bfloat16)
    routed = route_features(normed)
    query_terms = project_rows(routed, (query_weight,))
    kv_terms = jnp.einsum(
        "rsd,dc->rsc",
        lax.all_gather(routed, "yz", axis=0, tiled=True),
        kv_weight,
        preferred_element_type=jnp.float32,
    )
    terms = jnp.concatenate([query_terms, kv_terms], axis=2)
    received = heads_to_requests(terms).reshape(own_reqs, drafts, rank_count, terms.shape[2])
    queries = received[..., :query_cols].reshape(own_reqs, drafts, HEADS, HEAD_DIM)
    fresh = received[..., query_cols:].reshape(own_reqs, drafts, 2, KV_HEADS, HEAD_DIM)
    positions = cache_lengths[:, None] + jnp.arange(drafts, dtype=jnp.int32)[None, :]
    rotated = rotate(queries.astype(jnp.float32), positions).astype(jnp.bfloat16)
    new_keys = rotate(fresh[:, :, 0].astype(jnp.float32), positions).astype(jnp.bfloat16)
    new_values = fresh[:, :, 1]
    stored = self_keys.shape[1]
    stored_keys = self_keys.reshape(own_reqs, stored, KV_HEADS, HEAD_DIM)
    stored_values = self_values.reshape(own_reqs, stored, KV_HEADS, HEAD_DIM)
    stored_valid = jnp.arange(stored, dtype=jnp.int32)[None, None, :] < cache_lengths[:, None, None]
    stored_valid = jnp.broadcast_to(stored_valid, (own_reqs, drafts, stored))
    causal = (
        jnp.arange(drafts, dtype=jnp.int32)[None, :] <= jnp.arange(drafts, dtype=jnp.int32)[:, None]
    )
    causal = causal[None]
    scores = jnp.concatenate(
        [head_scores(rotated, stored_keys, stored_valid), head_scores(rotated, new_keys, causal)],
        axis=-1,
    )
    probs = normalize_scores(scores)
    mixed = jnp.einsum(
        "rkgst,rtkd->rskgd", probs[..., :stored], stored_values, preferred_element_type=jnp.float32
    )
    mixed = mixed + jnp.einsum(
        "rkgst,rtkd->rskgd", probs[..., stored:], new_values, preferred_element_type=jnp.float32
    )
    attended = mixed.astype(jnp.bfloat16).reshape(own_reqs, drafts, HEADS * HEAD_DIM)
    middle = (hidden.astype(jnp.float32) + rows_out(attended, out_weight)).astype(jnp.bfloat16)
    cross_normed = rms_scale(middle.astype(jnp.float32), cross_norm_gain).astype(jnp.bfloat16)
    cross_routed = route_features(cross_normed)
    cross_terms = project_rows(cross_routed, (cross_query_weight,))
    cross_queries = heads_to_requests(cross_terms).reshape(own_reqs, drafts, HEADS, HEAD_DIM)
    normed_queries = rms_scale(cross_queries.astype(jnp.float32), query_gain).astype(jnp.bfloat16)
    slots = image_keys.shape[1]
    image_valid = jnp.arange(slots, dtype=jnp.int32)[None, None, :] < image_counts[:, None, None]
    image_valid = jnp.broadcast_to(image_valid, (own_reqs, drafts, slots))
    cross_probs = normalize_scores(
        head_scores(
            normed_queries, image_keys.reshape(own_reqs, slots, KV_HEADS, HEAD_DIM), image_valid
        )
    )
    cross_mixed = jnp.einsum(
        "rkgst,rtkd->rskgd",
        cross_probs,
        image_values.reshape(own_reqs, slots, KV_HEADS, HEAD_DIM),
        preferred_element_type=jnp.float32,
    )
    cross_attended = cross_mixed.astype(jnp.bfloat16).reshape(own_reqs, drafts, HEADS * HEAD_DIM)
    cross_projected = rows_out(cross_attended, cross_out_weight)
    layer_out = middle.astype(jnp.float32) + jnp.tanh(cross_gate[0]) * cross_projected
    return layer_out.astype(jnp.bfloat16)


LANES = 128
TILE = 16
BF16 = jnp.bfloat16
F32 = jnp.float32


def layer_kernel(
    nz,
    nx,
    drafts,
    lengths_ref,
    counts_ref,
    gate_ref,
    hidden_ref,
    gain_ref,
    cross_gain_ref,
    query_gain_ref,
    cos_ref,
    sin_ref,
    self_keys_ref,
    self_values_ref,
    image_keys_ref,
    image_values_ref,
    wq_ref,
    wkv_ref,
    wo_ref,
    wcq_ref,
    wco_ref,
    out_ref,
    wq,
    wkv,
    wo,
    wcq,
    wco,
    keys,
    values,
    ikeys,
    ivalues,
    hid,
    mid,
    wide,
    lhs,
    rows_out_buf,
    rows_in,
    part_out,
    part_in,
    total,
    tile_f,
    tile_b,
    route_b,
    heads_f,
    heads_b,
    load_sem,
    scat_send,
    scat_recv,
    part_send,
    part_recv,
    route_send,
    route_recv,
):
    n = nz * nx
    j = lax.axis_index("yz")
    i = lax.axis_index("gx")
    me = j * nx + i
    chunks = hid.shape[0] // drafts
    block = chunks // nx
    cols = wo.shape[1] // nx
    per = cols // LANES
    slots = self_keys_ref.shape[0]

    def place(d):
        return {"yz": d // nx, "gx": d % nx}

    loads = [
        (wq_ref, wq),
        (wkv_ref, wkv),
        (self_keys_ref, keys.at[pl.ds(0, slots)]),
        (self_values_ref, values.at[pl.ds(0, slots)]),
        (wo_ref, wo),
        (wcq_ref, wcq),
        (image_keys_ref, ikeys),
        (image_values_ref, ivalues),
        (wco_ref, wco),
    ]
    copies = [pltpu.make_async_copy(a, b, load_sem.at[k]) for k, (a, b) in enumerate(loads)]
    copies[0].start()
    copies[1].start()

    barrier = pltpu.get_barrier_semaphore()

    def greet(k, _):
        pl.semaphore_signal(
            barrier, inc=1, device_id=place((me + k) % n), device_id_type=pl.DeviceIdType.MESH
        )
        return 0

    lax.fori_loop(1, n, greet, 0, unroll=True)

    def norm_rows(rows, gain):
        scaled = []
        for s in range(drafts):
            x = rows[s * chunks : (s + 1) * chunks, :]
            mean = jnp.sum(jnp.sum(x * x, axis=0, keepdims=True), axis=1, keepdims=True) / (
                chunks * LANES
            )
            scaled.append(x * lax.rsqrt(mean + 1e-05) * gain)
        return scaled

    def far_first(k):
        return (k + n // 2 - 2) % (n - 1) + 1

    def scatter_copy(stage, k, source, target):
        d = (me + k) % n
        return pltpu.make_async_remote_copy(
            src_ref=rows_out_buf.at[stage, :, pl.ds(pl.multiple_of((source % nx) * block, block), block)],
            dst_ref=rows_in.at[stage, target],
            send_sem=scat_send.at[stage],
            recv_sem=scat_recv.at[stage],
            device_id=place(d),
            device_id_type=pl.DeviceIdType.MESH,
        )

    def scatter(stage):
        def send(k, _):
            k = far_first(k)
            scatter_copy(stage, k, (me + k) % n, me).start()
            return 0

        lax.fori_loop(1, n, send, 0, unroll=True)

    def all_rows(stage, sems):
        every = rows_in.at[stage, pl.ds(0, n - 1)]
        pltpu.make_async_copy(every, every, sems.at[stage]).wait()

    def all_tiles(stage, sems):
        every = route_b.at[stage, pl.ds(0, n - 1)]
        pltpu.make_async_copy(every, every, sems.at[stage]).wait()

    def gather(stage):
        rows = drafts * block
        own = rows_out_buf[stage, :, pl.ds(pl.multiple_of(i * block, block), block), :]
        wide[pl.ds(pl.multiple_of(me * rows, TILE), rows), :] = own.reshape(rows, LANES).astype(F32)

        all_rows(stage, scat_recv)

        def widen(k, _):
            source = (me - k + n) % n
            got = rows_in[stage, source]
            wide[pl.ds(pl.multiple_of(source * rows, TILE), rows), :] = got.reshape(
                rows, LANES
            ).astype(F32)
            return 0

        lax.fori_loop(1, n, widen, 0, unroll=True)
        for s in range(drafts):
            for c in range(block):
                lhs[s * n : (s + 1) * n, c * LANES : (c + 1) * LANES] = wide[
                    pl.ds(s * block + c, n, stride=rows), :
                ].astype(BF16)

    across_chip = (1 - i // 2) * 2
    same_chip = i // 2 * 2
    other_core = 1 - i % 2
    peers = (same_chip + other_core, across_chip + i % 2, same_chip + other_core)

    def part_copy(stage, step, width, target):
        return pltpu.make_async_remote_copy(
            src_ref=part_out.at[stage, step, :, pl.ds(0, width)],
            dst_ref=part_in.at[stage, step, :, pl.ds(0, width)],
            send_sem=part_send.at[stage, step],
            recv_sem=part_recv.at[stage, step],
            device_id={"gx": target},
            device_id_type=pl.DeviceIdType.MESH,
        )

    def project(stage, weights):
        width = sum(w.shape[1] // nx for w in weights)

        def piece(target):
            return [
                jnp.dot(
                    lhs[...],
                    w[:, pl.ds(pl.multiple_of(target * (w.shape[1] // nx), LANES), w.shape[1] // nx)],
                    preferred_element_type=F32,
                )
                for w in weights
            ]

        def store(ref, target):
            at = 0
            for term in piece(target):
                ref[:, at : at + term.shape[1]] = term
                at += term.shape[1]

        def link(step):
            return part_copy(stage, step, width, peers[step])

        store(part_out.at[stage, 0], across_chip + other_core)
        link(0).start()
        store(part_out.at[stage, 1], across_chip + i % 2)
        link(0).wait_recv()
        part_out[stage, 1, :, :width] += part_in[stage, 0, :, :width]
        link(1).start()
        store(part_out.at[stage, 2], peers[2])
        link(2).start()
        store(total, i)
        link(2).wait_recv()
        total[:, :width] += part_in[stage, 2, :, :width]
        link(1).wait_recv()
        total[:, :width] += part_in[stage, 1, :, :width]
        return width // LANES

    def route_copy(stage, buf_out, buf_in, k, source, target):
        return pltpu.make_async_remote_copy(
            src_ref=buf_out.at[source],
            dst_ref=buf_in.at[target],
            send_sem=route_send.at[stage],
            recv_sem=route_recv.at[stage],
            device_id=place((me + k) % n),
            device_id_type=pl.DeviceIdType.MESH,
        )

    def route(stage, heads, finish=lambda rows: rows):
        buf_out, buf_in = tile_b.at[stage], route_b.at[stage]
        for s in range(drafts):
            for h in range(heads):
                tile_f[pl.ds(s * heads + h, n, stride=TILE), :] = total[
                    s * n : (s + 1) * n, h * LANES : (h + 1) * LANES
                ]
        buf_out[...] = finish(tile_f[...]).reshape(n, TILE, LANES).astype(BF16)
        exchange(stage)
        collect(stage)

    def exchange(stage):
        buf_out, buf_in = tile_b.at[stage], route_b.at[stage]

        def send(k, _):
            k = far_first(k)
            route_copy(stage, buf_out, buf_in, k, (me + k) % n, me).start()
            return 0

        lax.fori_loop(1, n, send, 0, unroll=True)
        buf_in[me] = buf_out[me]

    def collect(stage):
        all_tiles(stage, route_recv)

    def attend(stage, kref, vref, kv_heads, valid, heads):
        tiles = n // kv_heads
        height = tiles * TILE
        scores = []
        for k in range(kv_heads):
            part = lax.dot_general(
                heads_b[k * height : (k + 1) * height, :],
                kref[:, k * LANES : (k + 1) * LANES],
                (((1,), (1,)), ((), ())),
                preferred_element_type=F32,
            )
            scores.append(jnp.where(valid, part * LANES ** (-0.5), -jnp.inf))
        scores = jnp.concatenate(scores, axis=0)
        weights = jnp.exp(scores - jnp.max(scores, axis=-1, keepdims=True))
        probs = (weights / jnp.sum(weights, axis=-1, keepdims=True)).astype(BF16)
        for k in range(kv_heads):
            heads_f[k * height : (k + 1) * height, :] = jnp.dot(
                probs[k * height : (k + 1) * height, :],
                vref[:, k * LANES : (k + 1) * LANES],
                preferred_element_type=F32,
            )
        for s in range(drafts):
            for d in range(n):
                at = s * chunks + d * per
                wide[at : at + per, :] = heads_f[
                    d * TILE + s * heads : d * TILE + s * heads + per, :
                ]
        rows_out_buf[stage] = (
            wide[: drafts * chunks, :].reshape(drafts, chunks, LANES).astype(BF16)
        )

    def from_tiles(stage, ref):
        heads_f[...] = route_b[stage].reshape(n * TILE, LANES).astype(F32)
        for s in range(drafts):
            for d in range(n):
                ref[s * chunks + d * per : s * chunks + (d + 1) * per, :] = heads_f[
                    d * TILE + s * per : d * TILE + (s + 1) * per, :
                ]

    for c in range(chunks):
        hid[pl.ds(c, drafts, stride=chunks), :] = hidden_ref[
            :, c * LANES : (c + 1) * LANES
        ].astype(F32)
    for s, x in enumerate(norm_rows(hid, gain_ref[...])):
        rows_out_buf[0, s] = x.astype(BF16)
    tile_f[...] = jnp.zeros_like(tile_f)
    pl.semaphore_wait(barrier, n - 1)
    scatter(0)
    for s in range(drafts):
        for d in range(n):
            tile_f[d * TILE + s * per : d * TILE + (s + 1) * per, :] = hid[
                s * chunks + d * per : s * chunks + (d + 1) * per, :
            ]
    tile_b[4] = tile_f[...].reshape(n, TILE, LANES).astype(BF16)
    exchange(4)
    tile_f[...] = jnp.zeros_like(tile_f)
    for copy in copies[2:]:
        copy.start()
    pad = keys.shape[0] - slots
    keys[slots:, :] = jnp.zeros((pad, keys.shape[1]), BF16)
    values[slots:, :] = jnp.zeros((pad, values.shape[1]), BF16)

    gather(0)
    copies[0].wait()
    copies[1].wait()
    heads = project(0, (wq, wkv))
    route(0, heads)
    got = route_b[0].reshape(n * TILE, LANES).astype(F32)
    cosine = jnp.concatenate([cos_ref[...]] * n, axis=0)
    sine = jnp.concatenate([sin_ref[...]] * n, axis=0)
    heads_b[...] = (got * cosine + pltpu.roll(got, LANES // 2, 1) * sine).astype(BF16)
    copies[2].wait()
    copies[3].wait()
    kv_heads = n // 2
    for k in range(kv_heads):
        lanes = slice(k * LANES, (k + 1) * LANES)
        keys[slots : slots + TILE, lanes] = heads_b[k * TILE : (k + 1) * TILE, :]
        values[slots : slots + TILE, lanes] = route_b[0, kv_heads + k]
    shape = (n // kv_heads * TILE, keys.shape[0])
    row = lax.broadcasted_iota(jnp.int32, shape, 0) % TILE
    column = lax.broadcasted_iota(jnp.int32, shape, 1)
    valid = column < lengths_ref[0]
    for s in range(drafts):
        valid = valid | ((column == slots + s * heads + per) & (row >= s * heads))
    attend(1, keys, values, kv_heads, valid, heads)
    scatter(1)
    gather(1)
    copies[4].wait()
    heads = project(1, (wo,))
    tile_f[...] = jnp.zeros_like(tile_f)
    collect(4)
    route(
        1, heads, lambda rows: rows + route_b[4].reshape(n * TILE, LANES).astype(F32)
    )
    from_tiles(1, mid)

    for s, x in enumerate(norm_rows(mid, cross_gain_ref[...])):
        rows_out_buf[2, s] = x.astype(BF16)
    scatter(2)
    gather(2)
    copies[5].wait()
    heads = project(2, (wcq,))
    route(2, heads)
    got = route_b[2].reshape(n * TILE, LANES).astype(F32)
    scale = lax.rsqrt(jnp.mean(got * got, axis=-1, keepdims=True) + 1e-05)
    heads_b[...] = (got * scale * query_gain_ref[...]).astype(BF16)
    copies[6].wait()
    copies[7].wait()
    shape = (n // kv_heads * TILE, ikeys.shape[0])
    valid = lax.broadcasted_iota(jnp.int32, shape, 1) < counts_ref[0]
    attend(3, ikeys, ivalues, kv_heads, valid, heads)
    scatter(3)
    gather(3)
    copies[8].wait()
    heads = project(3, (wco,))
    gate = jnp.tanh(jnp.full((1, LANES), gate_ref[0], F32))
    route(
        3,
        heads,
        lambda rows: tile_b[1].reshape(n * TILE, LANES).astype(F32) + gate * rows,
    )
    from_tiles(3, mid)
    for c in range(chunks):
        out_ref[:, c * LANES : (c + 1) * LANES] = mid[
            pl.ds(c, drafts, stride=chunks), :
        ].astype(BF16)

    all_tiles(4, route_send)
    for stage in range(4):
        all_rows(stage, scat_send)
        all_tiles(stage, route_send)
        width = total.shape[1] if stage == 0 else cols
        for step in range(nx - 1):
            part_copy(stage, step, width, peers[step]).wait_send()


def shards_by_kernel(
    hidden,
    cache_lengths,
    image_counts,
    self_keys,
    self_values,
    image_keys,
    image_values,
    norm_gain,
    query_weight,
    kv_weight,
    out_weight,
    cross_norm_gain,
    cross_query_weight,
    query_gain,
    cross_out_weight,
    cross_gate,
):
    nz, nx = lax.axis_size("yz"), lax.axis_size("gx")
    n = nz * nx
    drafts, model = hidden.shape[1], hidden.shape[2]
    chunks = model // LANES
    cols = query_weight.shape[1] // nx
    width = cols + kv_weight.shape[1] // nx
    per = width // LANES
    position = cache_lengths[0] + jnp.minimum(jnp.arange(TILE, dtype=jnp.int32) // per, drafts - 1)
    half_dim = HEAD_DIM // 2
    freqs = 500000.0 ** (-2.0 * jnp.arange(half_dim, dtype=F32) / HEAD_DIM)
    angles = position.astype(F32)[:, None] * freqs
    cosine, sine = jnp.cos(angles), jnp.sin(angles)
    cosine = jnp.concatenate([cosine, cosine], axis=1)
    sine = jnp.concatenate([-sine, sine], axis=1)
    slots, kv_width = self_keys.shape[1], self_keys.shape[2]
    images = image_keys.shape[1]
    rows = drafts * n
    vmem = pl.BlockSpec(memory_space=pltpu.VMEM)
    smem = pl.BlockSpec(memory_space=pltpu.SMEM)
    away = pl.BlockSpec(memory_space=pl.ANY)
    out = pl.pallas_call(
        functools.partial(layer_kernel, nz, nx, drafts),
        out_shape=jax.ShapeDtypeStruct((drafts, model), BF16),
        in_specs=[smem] * 3 + [vmem] * 6 + [away] * 9,
        out_specs=vmem,
        scratch_shapes=[
            pltpu.VMEM(query_weight.shape, BF16),
            pltpu.VMEM(kv_weight.shape, BF16),
            pltpu.VMEM(out_weight.shape, BF16),
            pltpu.VMEM(cross_query_weight.shape, BF16),
            pltpu.VMEM(cross_out_weight.shape, BF16),
            pltpu.VMEM((slots + LANES, kv_width), BF16),
            pltpu.VMEM((slots + LANES, kv_width), BF16),
            pltpu.VMEM((images, kv_width), BF16),
            pltpu.VMEM((images, kv_width), BF16),
            pltpu.VMEM((drafts * chunks, LANES), F32),
            pltpu.VMEM((drafts * chunks, LANES), F32),
            pltpu.VMEM((n * drafts * (chunks // nx), LANES), F32),
            pltpu.VMEM((rows, model // nx), BF16),
            pltpu.VMEM((4, drafts, chunks, LANES), BF16),
            pltpu.VMEM((4, n, drafts, chunks // nx, LANES), BF16),
            pltpu.VMEM((4, nx - 1, rows, width), F32),
            pltpu.VMEM((4, nx - 1, rows, width), F32),
            pltpu.VMEM((rows, width), F32),
            pltpu.VMEM((n * TILE, LANES), F32),
            pltpu.VMEM((5, n, TILE, LANES), BF16),
            pltpu.VMEM((5, n, TILE, LANES), BF16),
            pltpu.VMEM((n * TILE, LANES), F32),
            pltpu.VMEM((n * TILE, LANES), BF16),
            pltpu.SemaphoreType.DMA((9,)),
            pltpu.SemaphoreType.DMA((4,)),
            pltpu.SemaphoreType.DMA((4,)),
            pltpu.SemaphoreType.DMA((4, nx - 1)),
            pltpu.SemaphoreType.DMA((4, nx - 1)),
            pltpu.SemaphoreType.DMA((5,)),
            pltpu.SemaphoreType.DMA((5,)),
        ],
        compiler_params=pltpu.CompilerParams(
            collective_id=0, has_side_effects=True, vmem_limit_bytes=56 * 2**20
        ),
        cost_estimate=pl.CostEstimate(
            flops=2 * rows * query_weight.shape[0] * (4 * query_weight.shape[1] + kv_weight.shape[1]),
            bytes_accessed=2 * query_weight.shape[0] * (4 * query_weight.shape[1] + kv_weight.shape[1]),
            transcendentals=0,
        ),
    )(
        cache_lengths,
        image_counts,
        cross_gate,
        hidden.reshape(drafts, model),
        norm_gain.reshape(chunks, LANES),
        cross_norm_gain.reshape(chunks, LANES),
        query_gain.reshape(1, HEAD_DIM),
        cosine,
        sine,
        self_keys.reshape(slots, kv_width),
        self_values.reshape(slots, kv_width),
        image_keys.reshape(images, kv_width),
        image_values.reshape(images, kv_width),
        query_weight,
        kv_weight,
        out_weight,
        cross_query_weight,
        cross_out_weight,
    )
    return out.reshape(hidden.shape)


def fits_kernel(hidden, kv_weight, query_weight):
    nx = lax.axis_size("gx")
    n = lax.axis_size("yz") * nx
    per = query_weight.shape[1] // nx // HEAD_DIM
    return (
        hidden.shape[0] == 1
        and n == 2 * KV_HEADS
        and nx == 4
        and query_weight.shape[1] == nx * per * HEAD_DIM
        and per * n == HEADS
        and kv_weight.shape[1] == nx * HEAD_DIM
        and hidden.shape[1] * (per + 1) <= TILE
        and query_weight.shape[0] % (TILE * LANES) == 0
    )


def shards(hidden, *rest):
    if fits_kernel(hidden, rest[8], rest[7]):
        return shards_by_kernel(hidden, *rest)
    return shards_by_collectives(hidden, *rest)


def solution(mesh):
    placed = (
        P(("grp", "yz", "gx"), None, None),
        P(("grp", "yz", "gx")),
        P(("grp", "yz", "gx")),
        P(("grp", "yz", "gx"), None, None),
        P(("grp", "yz", "gx"), None, None),
        P(("grp", "yz", "gx"), None, None),
        P(("grp", "yz", "gx"), None, None),
        P(),
        P("gx", "yz"),
        P("gx", "yz"),
        P("gx", "yz"),
        P(),
        P("gx", "yz"),
        P(),
        P("gx", "yz"),
        P(),
    )
    return jax.shard_map(
        shards,
        mesh=mesh,
        in_specs=placed,
        out_specs=P(("grp", "yz", "gx"), None, None),
        check_vma=False,
    )
```
